512 devices in a mesh: grp: 16 (over z, core), inner: 32 (over x, y).
Axes of the slice: x: 4, y: 8, z: 8, core: 2. Of those that a mesh axis runs over, the one named last changes fastest.
Arguments:
- queries: bfloat16 [256, 64, 192], P('inner', 'grp'), may hold values from -300 to 300
- tenant_ids: int32 [256], replicated, may hold values from 0 to 3
- prefix_lengths: int32 [4], replicated, may hold values from 2 to 4096, as said below
- latent_cache: bfloat16 [4096, 576], P('inner'), may hold values from -8 to 8
- key_absorb: bfloat16 [64, 128, 512], P('grp'), may hold values from -0.5 to 0.5
- value_absorb: bfloat16 [64, 512, 128], P('grp'), may hold values from -12 to 12
- key_down: bfloat16 [4, 64, 128, 16], P(None, 'grp'), may hold values from -0.5 to 0.5
- key_up: bfloat16 [4, 64, 16, 512], P(None, 'grp'), may hold values from -1.5 to 1.5
- value_down: bfloat16 [4, 64, 512, 16], P(None, 'grp'), may hold values from -6 to 6
- value_up: bfloat16 [4, 64, 16, 128], P(None, 'grp'), may hold values from -1.5 to 1.5
- out_proj: bfloat16 [8192, 7168], P('grp', 'inner'), may hold values from -0.0625 to 0.0625
Outputs:
- attended: bfloat16 [256, 7168], P('grp', 'inner')
The draws below stay inside these ranges and needn't reach their ends.
Inputs may be any that keep to these rules, and one draw needn't show every extreme that they name: `prefix_lengths`: at least one tenant sees all 4096 positions.
All inputs are finite; a program needn't handle non-finite values.
Results may differ from the reference program's by a relative error of at most 0.011.
Values may be sent and summed in bfloat16 or wider, within the bound.
A program may use at most 64 MiB of HBM per device.

```python
import jax
import jax.numpy as jnp
from jax import lax

D = 7168
HEADS = 64
LAT = 512
ROPE = 64
NOPE = 128
VDIM = 128
RANK = 16
TENANTS = 4
TQ = 256
CTX_DEV = 128
CTX = 4096
N_INNER = 32


def draw_latent_cache(key, part):
    inner_key = jax.random.fold_in(key, 23)
    values = jnp.clip(jax.random.normal(jax.random.fold_in(inner_key, 3), (CTX, LAT + ROPE), jnp.float32), -6.0, 6.0)
    return values.astype(jnp.bfloat16)


def draw_queries(key, part):
    inner_key = jax.random.fold_in(key, 41)
    values = jnp.clip(jax.random.normal(jax.random.fold_in(inner_key, 3), (TQ, HEADS, NOPE + ROPE), jnp.float32), -6.0, 6.0)
    return values.astype(jnp.bfloat16)


def draw_prefix_lengths(key, part):
    lengths = jax.random.randint(jax.random.fold_in(key, 31), (TENANTS,), 2, CTX + 1, jnp.int32)
    widest = jax.random.randint(jax.random.fold_in(key, 32), (), 0, TENANTS, jnp.int32)
    return jnp.where(jnp.arange(TENANTS, dtype=jnp.int32) == widest, CTX, lengths).astype(jnp.int32)


def plant(entries, key, low, largest):
    longest = entries.shape.index(max(entries.shape))
    spots = []
    for shift in (0, 1):
        where = [jax.random.randint(jax.random.fold_in(key, axis), (), 0, length) for axis, length in enumerate(entries.shape)]
        where[longest] = (where[longest] + shift) % entries.shape[longest]
        spots.append(tuple(where))
    return entries.at[spots[0]].set(low).at[spots[1]].set(largest)


def block_levels(key, dims, pieces, low, high):
    level, own = 1.0, jax.random.fold_in(key, 6)
    for axis_at, parts in pieces:
        heights = jnp.exp(jax.random.uniform(jax.random.fold_in(own, axis_at), (parts,), jnp.float32, low / len(pieces), high / len(pieces)))
        level = level * jnp.repeat(heights, dims[axis_at] // parts).reshape([-1 if axis == axis_at else 1 for axis in range(len(dims))])
    return level


def centred(key, shape, spread, limit, cuts=(), kind=jnp.bfloat16):
    loudness = block_levels(key, shape, cuts, -0.22, 0.18) if cuts else 1.0
    array = jax.random.normal(key, shape, jnp.float32) * spread * loudness
    return jnp.minimum(jnp.maximum(array, -limit), limit).astype(kind)


def setup_inputs(seed: int = 0) -> dict:
    seeds = jax.random.split(jax.random.key(seed), 12)
    queries = draw_queries(jax.random.fold_in(seeds[11], 71), 0)
    tenant_ids = plant(jax.random.randint(seeds[1], (TQ,), 0, TENANTS), jax.random.fold_in(seeds[1], 1), 0, TENANTS - 1).astype(jnp.int32)
    prefix_lengths = draw_prefix_lengths(jax.random.fold_in(seeds[11], 71), 0)
    latent_cache = draw_latent_cache(jax.random.fold_in(seeds[11], 71), 0)
    key_absorb = centred(seeds[4], (HEADS, NOPE, LAT), NOPE ** -0.5, 0.5, ((0, 16),))
    value_absorb = centred(seeds[5], (HEADS, LAT, VDIM), 2.0, 12.0, ((0, 16),))
    key_down = centred(seeds[6], (TENANTS, HEADS, NOPE, RANK), NOPE ** -0.5, 0.5, ((1, 16),))
    key_up = centred(seeds[7], (TENANTS, HEADS, RANK, LAT), RANK ** -0.5, 1.5, ((1, 16),))
    value_down = centred(seeds[8], (TENANTS, HEADS, LAT, RANK), 1.0, 6.0, ((1, 16),))
    value_up = centred(seeds[9], (TENANTS, HEADS, RANK, VDIM), RANK ** -0.5, 1.5, ((1, 16),))
    out_proj = centred(seeds[10], (HEADS * VDIM, D), (HEADS * VDIM) ** -0.5, 0.0625, ((0, 16), (1, 32)))
    return dict(queries=queries, tenant_ids=tenant_ids, prefix_lengths=prefix_lengths, latent_cache=latent_cache, key_absorb=key_absorb, value_absorb=value_absorb, key_down=key_down, key_up=key_up, value_down=value_down, value_up=value_up, out_proj=out_proj)


masked_score = -30000.0


def absorb(queries, chosen, key_absorb, key_down, key_up):
    nope_part = queries[:, :, :NOPE].astype(jnp.float32)
    rope_part = queries[:, :, NOPE:].astype(jnp.float32)
    latent = jnp.einsum("thn,hnc->thc", nope_part, key_absorb.astype(jnp.float32))
    lowrank = jnp.einsum("thn,khnr->thkr", nope_part, key_down.astype(jnp.float32)) * chosen[:, None, :, None]
    lowrank = lowrank.astype(jnp.bfloat16).astype(jnp.float32)
    latent = latent + jnp.einsum("thkr,khrc->thc", lowrank, key_up.astype(jnp.float32))
    return jnp.concatenate([latent, rope_part], axis=2).astype(jnp.bfloat16)


def reference(queries, tenant_ids, prefix_lengths, latent_cache, key_absorb, value_absorb, key_down, key_up, value_down, value_up, out_proj):
    table = tenant_ids[:, None] == jnp.arange(TENANTS, dtype=jnp.int32)[None, :]
    chosen = table.astype(jnp.float32)
    limits = jnp.sum(jnp.where(table, prefix_lengths[None, :], 0), axis=1).astype(jnp.int32)
    query_full = absorb(queries, chosen, key_absorb, key_down, key_up).astype(jnp.float32)
    scale = (NOPE + ROPE) ** -0.5

    def one_block(block):
        start = (block * CTX_DEV).astype(jnp.int32)
        cache_block = lax.dynamic_slice_in_dim(latent_cache, start, CTX_DEV, 0).astype(jnp.float32)
        scores = jnp.einsum("thc,jc->thj", query_full, cache_block) * scale
        positions = start + jnp.arange(CTX_DEV, dtype=jnp.int32)
        allowed = (positions[None, :] < limits[:, None])[:, None, :]
        masked = jnp.where(allowed, scores, masked_score)
        block_max = jnp.max(masked, axis=2)
        weights = jnp.where(allowed, jnp.exp(masked - block_max[:, :, None]), 0.0)
        block_sum = jnp.sum(weights, axis=2)
        rounded = weights.astype(jnp.bfloat16).astype(jnp.float32)
        block_latent = jnp.einsum("thj,jc->thc", rounded, cache_block[:, :LAT]).astype(jnp.bfloat16).astype(jnp.float32)
        values = jnp.einsum("thc,hcv->thv", block_latent, value_absorb.astype(jnp.float32))
        lowrank = jnp.einsum("thc,khcr->thkr", block_latent, value_down.astype(jnp.float32)) * chosen[:, None, :, None]
        lowrank = lowrank.astype(jnp.bfloat16).astype(jnp.float32)
        values = values + jnp.einsum("thkr,khrv->thv", lowrank, value_up.astype(jnp.float32))
        return block_max, block_sum, values

    block_max, block_sum, values = lax.map(one_block, jnp.arange(N_INNER, dtype=jnp.int32))
    peak = jnp.max(block_max, axis=0)
    factor = jnp.exp(block_max - peak[None])
    numer = jnp.sum(values * factor[..., None], axis=0)
    denom = jnp.sum(block_sum * factor, axis=0)
    head_out = (numer / denom[:, :, None]).astype(jnp.bfloat16)
    flat = head_out.reshape(TQ, HEADS * VDIM)
    return jnp.dot(flat, out_proj, preferred_element_type=jnp.float32).astype(jnp.bfloat16)
```

```python
import functools

import jax
import jax.numpy as jnp
from jax import lax
from jax.experimental import pallas as pl
from jax.experimental.pallas import tpu as pltpu
from jax.sharding import PartitionSpec as P

MESH = pl.DeviceIdType.MESH
BF, F32 = jnp.bfloat16, jnp.float32
LAT, ROPE, NOPE = 512, 64, 128
NX, NY, NG = 4, 8, 16
HEADS, TOK = 4, 8
SPAN = 128
MASKED = -30000.0
SCALE = (NOPE + ROPE) ** -0.5


def dot(a, b):
    return lax.dot_general(a, b, (((1,), (0,)), ((), ())), preferred_element_type=F32)


def dot_nt(a, b):
    return lax.dot_general(a, b, (((1,), (1,)), ((), ())), preferred_element_type=F32)


def kernel(
    q_hbm, ids_hbm, lim_hbm, lat_hbm, ka_hbm, va_hbm, kd_hbm, ku_hbm, vd_hbm, vu_hbm, wo_hbm,
    out_ref,
    q_v, q_n, q_r, ids_v, lim_s, lat, ka, va, kd, ku, vd, vu, wo,
    qbuf, qf, bl, vs, st, rv, rst, ho, zs, zr,
    lsem, q_ss, q_rs, l_ss, l_rs, v_ss, v_rs, s_ss, s_rs, y_ss, y_rs, x_ss, x_rs, z_ss, z_rs,
):
    g = lax.axis_index("grp")
    inner = lax.axis_index("inner")
    x, y = inner // NY, inner % NY

    def ypeer(d):
        return (y + d) % NY

    def xpeer(d):
        return (x + d) % NX

    def gpeer(d):
        return (g + d) % NG

    def remote(src, dst, ss, rs, to_g, to_inner):
        return pltpu.make_async_remote_copy(
            src_ref=src, dst_ref=dst, send_sem=ss, recv_sem=rs,
            device_id=(to_g, to_inner), device_id_type=MESH,
        )

    loads = {}
    for n, (name, src, dst) in enumerate((
        ("q", q_hbm, q_v), ("ids", ids_hbm, ids_v), ("lim", lim_hbm, lim_s), ("lat", lat_hbm, lat.at[x]),
        ("ka", ka_hbm, ka), ("kd", kd_hbm, kd), ("ku", ku_hbm, ku), ("va", va_hbm, va), ("vd", vd_hbm, vd),
        ("vu", vu_hbm, vu), ("wo", wo_hbm, wo),
    )):
        loads[name] = pltpu.make_async_copy(src, dst, lsem.at[n])
        loads[name].start()

    barrier = pltpu.get_barrier_semaphore()
    for d in range(1, NY):
        pl.semaphore_signal(barrier, 1, device_id=(g, x * NY + ypeer(d)), device_id_type=MESH)
    for d in range(1, NX):
        pl.semaphore_signal(barrier, 1, device_id=(g, xpeer(d) * NY + y), device_id_type=MESH)
    for d in range(1, NG):
        pl.semaphore_signal(barrier, 1, device_id=(gpeer(d), inner), device_id_type=MESH)

    loads["q"].wait()
    q32 = q_v[...].astype(F32)
    for t in range(TOK):
        q_n[t * HEADS : (t + 1) * HEADS, :] = q32[t, :, :NOPE]
        q_r[t * HEADS : (t + 1) * HEADS, :ROPE] = q32[t, :, NOPE:]
    rows = [q_n[pl.ds(h, TOK, stride=HEADS), :] for h in range(HEADS)]
    ropes = [q_r[pl.ds(h, TOK, stride=HEADS), :][:, :ROPE] for h in range(HEADS)]
    rows += [jnp.concatenate(ropes[h : h + 2], axis=1) for h in (0, 2)]
    qbuf[y] = jnp.concatenate(rows, axis=0).astype(BF)
    loads["lat"].wait()

    pl.semaphore_wait(barrier, NY - 1 + NX - 1 + NG - 1)

    sends = []
    order_y = (4, 3, 5, 2, 6, 1, 7)
    for d in order_y:
        sends.append(remote(qbuf.at[y], qbuf.at[y], q_ss.at[d], q_rs.at[y], g, x * NY + ypeer(d)))
        sends[-1].start()
    for d in (2, 1, 3):
        sends.append(remote(lat.at[x], lat.at[x], l_ss.at[d], l_rs.at[x], g, xpeer(d) * NY + y))
        sends[-1].start()

    loads["ids"].wait()
    loads["lim"].wait()
    span = NY * TOK
    wide = NX * span
    row = lax.broadcasted_iota(jnp.int32, (span, wide), 0)
    lane = lax.broadcasted_iota(jnp.int32, (span, wide), 1)
    tenant = jnp.sum(jnp.where(lane == row + x * span, ids_v[...], 0), axis=1, keepdims=True)
    limit = jnp.zeros_like(tenant)
    for k in range(4):
        limit = jnp.where(tenant == k, lim_s[k], limit)
    chosen = lax.broadcasted_iota(jnp.int32, (span, 64), 1) // 16 == tenant
    for name in ("ka", "kd", "ku", "va", "vd", "vu", "wo"):
        loads[name].wait()
    wo_all = jnp.concatenate([wo[...], jnp.zeros((32, LAT), BF)], axis=0)

    def arrived(dst, rs):
        remote(dst, dst, q_ss.at[0], rs, g, inner).wait_recv()

    for d in order_y:
        arrived(qbuf.at[ypeer(d)], q_rs.at[ypeer(d)])
    blocks = [qbuf[k].astype(F32) for k in range(NY)]
    half = lax.broadcasted_iota(jnp.int32, (span, NOPE), 1) // ROPE
    for h in range(HEADS):
        nope = jnp.concatenate([b[h * TOK : (h + 1) * TOK] for b in blocks], axis=0).astype(BF)
        first = HEADS * TOK + (h // 2) * TOK
        rope = jnp.concatenate([b[first : first + TOK] for b in blocks], axis=0)
        low = dot_nt(nope, kd[:, h].reshape(64, NOPE))
        low = jnp.where(chosen, low, 0.0).astype(BF)
        latent = dot(nope, ka[h]) + dot(low, ku[:, h].reshape(64, LAT))
        qf[h * span : (h + 1) * span, :LAT] = latent.astype(BF)
        qf[h * span : (h + 1) * span, LAT:] = jnp.where(half == h % 2, rope, 0.0).astype(BF)

    for d in (1, 3, 2):
        arrived(lat.at[xpeer(d)], l_rs.at[xpeer(d)])

    base = lax.broadcasted_iota(jnp.int32, (2 * span, SPAN), 1) + y * SPAN
    limit2 = jnp.concatenate([limit, limit], axis=0)
    eye = lax.broadcasted_iota(jnp.int32, (SPAN, SPAN), 0) == lax.broadcasted_iota(
        jnp.int32, (SPAN, SPAN), 1
    )
    for hp in range(2):
        mine = qf[hp * 2 * span : (hp + 1) * 2 * span, :]
        scores, okay = [], []
        for b in range(NX):
            keys = jnp.concatenate([lat[b], lat[b, LAT:]], axis=0)
            okay.append(base + b * NY * SPAN < limit2)
            scores.append(jnp.where(okay[b], dot(mine, keys) * SCALE, MASKED))
        top = functools.reduce(jnp.maximum, scores)
        top = jnp.max(top, axis=1, keepdims=True)
        weights = [jnp.where(ok, jnp.exp(s - top), 0.0) for ok, s in zip(okay, scores)]
        total = jnp.sum(functools.reduce(jnp.add, weights), axis=1, keepdims=True)
        acc = functools.reduce(
            jnp.add, [dot_nt(w.astype(BF), lat[b, :LAT]) for b, w in enumerate(weights)]
        )
        bl[...] = acc.astype(BF)
        st[hp, 0:1, :] = jnp.sum(jnp.where(eye, top, 0.0), axis=0, keepdims=True)
        st[hp, 1:2, :] = jnp.sum(jnp.where(eye, total, 0.0), axis=0, keepdims=True)
        for hl in range(2):
            h = hp * 2 + hl
            mine = bl[hl * span : (hl + 1) * span, :]
            low = dot_nt(mine, vd[:, h].reshape(64, LAT))
            low = jnp.where(chosen, low, 0.0).astype(BF)
            values = (dot(mine, va[h]) + dot(low, vu[:, h].reshape(64, NOPE))).astype(BF)
            for tb in range(4):
                vs[tb * 2 + hp, hl * 16 : (hl + 1) * 16, :] = values[tb * 16 : (tb + 1) * 16]

    for d in order_y:
        to = ypeer(d)
        sends.append(remote(vs.at[to], rv.at[y], v_ss.at[d], v_rs.at[y], g, x * NY + to))
        sends[-1].start()
        sends.append(remote(st.at[to % 2], rst.at[y], s_ss.at[d], s_rs.at[y], g, x * NY + to))
        sends[-1].start()
    rv[y] = vs[y]
    rst[y] = st[y % 2]
    for d in order_y:
        arrived(rst.at[ypeer(d)], s_rs.at[ypeer(d)])

    tops = [rst[k, 0:1, :] for k in range(NY)]
    peak = functools.reduce(jnp.maximum, tops)
    factors = [jnp.exp(t - peak) for t in tops]
    denom = functools.reduce(jnp.add, [f * rst[k, 1:2, :] for k, f in enumerate(factors)])
    r32 = lax.broadcasted_iota(jnp.int32, (32, SPAN), 0)
    l32 = lax.broadcasted_iota(jnp.int32, (32, SPAN), 1)
    pick = l32 == (r32 // 16) * span + (y // 2) * 16 + r32 % 16
    shares = [
        jnp.sum(jnp.where(pick, f / denom, 0.0), axis=1, keepdims=True) for f in factors
    ]
    for d in order_y:
        arrived(rv.at[ypeer(d)], v_rs.at[ypeer(d)])
    head = functools.reduce(jnp.add, [s * rv[k].astype(F32) for k, s in enumerate(shares)])
    ho[x, y] = jnp.concatenate([head[:16], head[16:]], axis=1).astype(BF)

    for d in order_y:
        sends.append(
            remote(ho.at[x, y], ho.at[x, y], y_ss.at[d], y_rs.at[y], g, x * NY + ypeer(d))
        )
        sends[-1].start()
    for d in order_y:
        arrived(ho.at[x, ypeer(d)], y_rs.at[ypeer(d)])
    for d in (2, 1, 3):
        sends.append(remote(ho.at[x], ho.at[x], x_ss.at[d], x_rs.at[x], g, xpeer(d) * NY + y))
        sends[-1].start()

    for e in (0, 1, 3, 2):
        xx = xpeer(e)
        if e:
            arrived(ho.at[xx], x_rs.at[xx])
        lhs = jnp.concatenate(
            [
                jnp.concatenate([ho[xx, 2 * tb], ho[xx, 2 * tb + 1]], axis=1)
                for tb in range(4)
            ],
            axis=0,
        )
        part = dot_nt(lhs, wo_all).astype(BF)
        for tb in range(4):
            zs[4 * xx + tb] = part[tb * 16 : (tb + 1) * 16]
    for d in (8, 9, 7, 6, 10, 5, 11, 4, 12, 3, 13, 2, 14, 15, 1):
        to = gpeer(d)
        sends.append(remote(zs.at[to], zr.at[g], z_ss.at[d], z_rs.at[g], to, inner))
        sends[-1].start()
    zr[g] = zs[g]
    for d in range(1, NG):
        arrived(zr.at[gpeer(d)], z_rs.at[gpeer(d)])
    whole = functools.reduce(jnp.add, [zr[k].astype(F32) for k in range(NG)])
    out_ref[...] = whole[:, : out_ref.shape[1]].astype(BF)
    for s in sends:
        s.wait_send()


def local(q, ids, limits, latent, ka, va, kd, ku, vd, vu, wo):
    args = (
        q, ids.reshape(1, -1), limits, latent.T, ka, va, kd.swapaxes(2, 3), ku,
        vd.swapaxes(2, 3), vu, wo.T,
    )
    sem = pltpu.SemaphoreType.DMA
    v = pltpu.VMEM
    return pl.pallas_call(
        kernel,
        out_shape=jax.ShapeDtypeStruct((q.shape[0] * 2, wo.shape[1]), BF),
        in_specs=[pl.BlockSpec(memory_space=pltpu.HBM)] * len(args),
        out_specs=pl.BlockSpec(memory_space=pltpu.VMEM),
        scratch_shapes=[
            v(q.shape, BF),
            v((TOK * HEADS, NOPE), F32),
            v((TOK * HEADS, NOPE), F32),
            v((1, ids.shape[0]), jnp.int32),
            pltpu.SMEM(limits.shape, jnp.int32),
            v((NX, LAT + ROPE, SPAN), BF),
            v(ka.shape, BF),
            v(va.shape, BF),
            v(args[6].shape, BF),
            v(ku.shape, BF),
            v(args[8].shape, BF),
            v(vu.shape, BF),
            v(args[10].shape, BF),
            v((NY, 48, 128), BF),
            v((HEADS * NY * TOK, LAT + 128), BF),
            v((2 * NY * TOK, LAT), BF),
            v((NY, 32, 128), BF),
            v((2, 8, 128), F32),
            v((NY, 32, 128), BF),
            v((NY, 8, 128), F32),
            v((NX, NY, 16, 256), BF),
            v((NG, 16, 256), BF),
            v((NG, 16, 256), BF),
            sem((len(args),)),
            *[sem((NY,))] * 2,
            *[sem((NX,))] * 2,
            *[sem((NY,))] * 6,
            *[sem((NX,))] * 2,
            *[sem((NG,))] * 2,
        ],
        compiler_params=pltpu.CompilerParams(
            collective_id=0, has_side_effects=True
        ),
    )(*args)


def solution(mesh):
    in_specs = (
        P("inner", "grp", None),
        P(),
        P(),
        P("inner", None),
        P("grp", None, None),
        P("grp", None, None),
        P(None, "grp", None, None),
        P(None, "grp", None, None),
        P(None, "grp", None, None),
        P(None, "grp", None, None),
        P("grp", "inner"),
    )
    return jax.shard_map(
        local, mesh=mesh, in_specs=in_specs, out_specs=P("grp", "inner"), check_vma=False
    )
```

```python
import functools

import jax
import jax.numpy as jnp
from jax import lax
from jax.experimental import pallas as pl
from jax.experimental.pallas import tpu as pltpu
from jax.sharding import PartitionSpec as P

MESH = pl.DeviceIdType.MESH
BF, F32 = jnp.bfloat16, jnp.float32
LAT, ROPE, NOPE = 512, 64, 128
NX, NY, NG = 4, 8, 16
HEADS, TOK = 4, 8
SPAN = 128
MASKED = -30000.0
FAR_Y, FAR_X = (4, 3, 5, 2, 6, 1, 7), (2, 1, 3)
SCALE = (NOPE + ROPE) ** -0.5


def dot(a, b):
    return lax.dot_general(a, b, (((1,), (0,)), ((), ())), preferred_element_type=F32)


def dot_nt(a, b):
    return lax.dot_general(a, b, (((1,), (1,)), ((), ())), preferred_element_type=F32)


def kernel(
    q_hbm, ids_hbm, lim_hbm, lat_hbm, ka_hbm, va_hbm, kd_hbm, ku_hbm, vd_hbm, vu_hbm, wo_hbm,
    z_out,
    q_v, q_n, q_r, ids_v, lim_s, lat, ka, va, kd, ku, vd, vu, wo,
    qbuf, qf, vs, rv, ho, zs,
    lsem, q_ss, q_rs, l_ss, l_rs, c_ss, c_rs, v_ss, v_rs, y_ss, y_rs, x_ss, x_rs, z_ss, z_rs,
):
    g = lax.axis_index("grp")
    inner = lax.axis_index("inner")
    x, y = inner // NY, inner % NY

    def ypeer(d):
        return (y + d) % NY

    def xpeer(d):
        return (x + d) % NX

    def gpeer(d):
        return (g + d) % NG

    def remote(src, dst, ss, rs, to_g, to_inner):
        return pltpu.make_async_remote_copy(
            src_ref=src, dst_ref=dst, send_sem=ss, recv_sem=rs,
            device_id=(to_g, to_inner), device_id_type=MESH,
        )

    def load(n, src, dst):
        copy = pltpu.make_async_copy(src, dst, lsem.at[n])
        copy.start()
        return copy

    def arrived(dst, rs):
        remote(dst, dst, q_ss.at[0], rs, g, inner).wait_recv()

    sends = []

    def send(*what):
        copy = remote(*what)
        copy.start()
        sends.append(copy)

    get_q = load(0, q_hbm, q_v)
    get_lat = load(1, lat_hbm, lat.at[x])
    barrier = pltpu.get_barrier_semaphore()
    for d in FAR_Y:
        pl.semaphore_signal(barrier, 1, device_id=(g, x * NY + ypeer(d)), device_id_type=MESH)
    for d in FAR_X:
        pl.semaphore_signal(barrier, 1, device_id=(g, xpeer(d) * NY + y), device_id_type=MESH)
    for d in range(1, NG):
        pl.semaphore_signal(barrier, 1, device_id=(gpeer(d), inner), device_id_type=MESH)

    get_q.wait()
    q32 = q_v[...].astype(F32)
    for t in range(TOK):
        q_n[t * HEADS : (t + 1) * HEADS, :] = q32[t, :, :NOPE]
        q_r[t * HEADS : (t + 1) * HEADS, :ROPE] = q32[t, :, NOPE:]
    rows = [q_n[pl.ds(h, TOK, stride=HEADS), :] for h in range(HEADS)]
    ropes = [q_r[pl.ds(h, TOK, stride=HEADS), :][:, :ROPE] for h in range(HEADS)]
    rows += [jnp.concatenate(ropes[h : h + 2], axis=1) for h in (0, 2)]
    qbuf[y] = jnp.concatenate(rows, axis=0).astype(BF)
    get_lat.wait()

    pl.semaphore_wait(barrier, NY - 1 + NX - 1 + NG - 1)

    for d in FAR_Y:
        send(qbuf.at[y], qbuf.at[y], q_ss.at[d], q_rs.at[y], g, x * NY + ypeer(d))
    part = pl.ds(pl.multiple_of((g % 2) * 288, 16), 288)
    for d in FAR_X:
        piece = lat.at[x, part]
        send(piece, piece, l_ss.at[d], l_rs.at[x], g, xpeer(d) * NY + y)
    get = [
        load(n + 2, src, dst)
        for n, (src, dst) in enumerate((
            (ids_hbm, ids_v), (lim_hbm, lim_s), (ka_hbm, ka), (kd_hbm, kd), (ku_hbm, ku), (va_hbm, va),
            (vd_hbm, vd), (vu_hbm, vu), (wo_hbm, wo.at[: wo_hbm.shape[0]]),
        ))
    ]

    wo[wo_hbm.shape[0] :, :] = jnp.zeros((wo.shape[0] - wo_hbm.shape[0], LAT), BF)
    for copy in get:
        copy.wait()
    span = NY * TOK
    wide = NX * span
    row = lax.broadcasted_iota(jnp.int32, (span, wide), 0)
    lane = lax.broadcasted_iota(jnp.int32, (span, wide), 1)
    tenant = jnp.sum(jnp.where(lane == row + x * span, ids_v[...], 0), axis=1, keepdims=True)
    limit = jnp.zeros_like(tenant)
    for k in range(4):
        limit = jnp.where(tenant == k, lim_s[k], limit)
    chosen = lax.broadcasted_iota(jnp.int32, (span, 64), 1) // 16 == tenant

    for d in FAR_Y:
        arrived(qbuf.at[ypeer(d)], q_rs.at[ypeer(d)])
    core = g + 1 - 2 * (g % 2)
    for d in (1, 3, 2):
        piece = lat.at[xpeer(d), part]
        arrived(piece, l_rs.at[xpeer(d)])
        send(piece, piece, c_ss.at[d], c_rs.at[d], core, inner)

    blocks = [qbuf[k].astype(F32) for k in range(NY)]
    half = lax.broadcasted_iota(jnp.int32, (span, NOPE), 1) // ROPE
    for h in range(HEADS):
        nope = jnp.concatenate([b[h * TOK : (h + 1) * TOK] for b in blocks], axis=0).astype(BF)
        first = HEADS * TOK + (h // 2) * TOK
        rope = jnp.concatenate([b[first : first + TOK] for b in blocks], axis=0)
        low = dot_nt(nope, kd[:, h].reshape(64, NOPE))
        low = jnp.where(chosen, low, 0.0).astype(BF)
        latent = dot(nope, ka[h]) + dot(low, ku[:, h].reshape(64, LAT))
        rows = pl.ds((h % 2) * span, span)
        qf[h // 2, rows, :LAT] = latent.astype(BF)
        qf[h // 2, rows, LAT:] = jnp.where(half == h % 2, rope, 0.0).astype(BF)

    other = pl.ds(pl.multiple_of((1 - g % 2) * 288, 16), 288)
    for d in (1, 3, 2):
        arrived(lat.at[xpeer(d), other], c_rs.at[d])

    base = lax.broadcasted_iota(jnp.int32, (2 * span, SPAN), 1) + y * SPAN
    limit2 = jnp.concatenate([limit, limit], axis=0)
    eye = lax.broadcasted_iota(jnp.int32, (SPAN, SPAN), 0) == lax.broadcasted_iota(
        jnp.int32, (SPAN, SPAN), 1
    )
    okay = [base + b * NY * SPAN < limit2 for b in range(NX)]
    for turn, peers in enumerate(((4, 2, 6, 0), (3, 5, 1, 7))):
        hp = (y + turn) % 2
        mine = qf[hp]
        scores = []
        for b in range(NX):
            keys = jnp.concatenate([lat[b], lat[b, LAT:]], axis=0)
            scores.append(jnp.where(okay[b], dot(mine, keys) * SCALE, MASKED))
        top = functools.reduce(jnp.maximum, scores)
        top = jnp.max(top, axis=1, keepdims=True)
        weights = [jnp.where(ok, jnp.exp(s - top), 0.0) for ok, s in zip(okay, scores)]
        total = jnp.sum(functools.reduce(jnp.add, weights), axis=1, keepdims=True)
        acc = functools.reduce(
            jnp.add, [dot_nt(w.astype(BF), lat[b, :LAT]) for b, w in enumerate(weights)]
        ).astype(BF)
        three = []
        for column in (top, total):
            rest = jnp.sum(jnp.where(eye, column, 0.0), axis=0, keepdims=True)
            for _ in range(3):
                three.append(rest.astype(BF).astype(F32))
                rest = rest - three[-1]
        three = jnp.concatenate(three + [jnp.zeros((10, SPAN), F32)], axis=0).astype(BF)
        values = []
        for hl in range(2):
            h = hp * 2 + hl
            mine = acc[hl * span : (hl + 1) * span, :]
            low = dot_nt(mine, vd[:, h].reshape(64, LAT))
            low = jnp.where(chosen, low, 0.0).astype(BF)
            values.append((dot(mine, va[h]) + dot(low, vu[:, h].reshape(64, NOPE))).astype(BF))
        for tb in range(4):
            vs[tb * 2 + hp] = jnp.concatenate(
                [values[0][tb * 16 : (tb + 1) * 16], values[1][tb * 16 : (tb + 1) * 16], three], axis=0
            )
        for d in peers:
            if d:
                to = ypeer(d)
                send(vs.at[to], rv.at[NY - d], v_ss.at[d], v_rs.at[NY - d], g, x * NY + to)
            else:
                rv[0] = vs[y]

    r32 = lax.broadcasted_iota(jnp.int32, (32, SPAN), 0)
    l32 = lax.broadcasted_iota(jnp.int32, (32, SPAN), 1)
    pick = l32 == (r32 // 16) * span + (y // 2) * 16 + r32 % 16
    for d in (2, 6, 4, 1, 7, 3, 5):
        arrived(rv.at[d], v_rs.at[d])
    tops, totals = [], []
    for k in range(NY):
        three = rv[k, 32:48, :].astype(F32)
        tops.append(three[0:1] + three[1:2] + three[2:3])
        totals.append(three[3:4] + three[4:5] + three[5:6])
    peak = functools.reduce(jnp.maximum, tops)
    factors = [jnp.exp(t - peak) for t in tops]
    denom = functools.reduce(jnp.add, [f * t for f, t in zip(factors, totals)])
    shares = [
        jnp.sum(jnp.where(pick, f / denom, 0.0), axis=1, keepdims=True) for f in factors
    ]
    head = functools.reduce(
        jnp.add, [s * rv[k, :32, :].astype(F32) for k, s in enumerate(shares)]
    )
    ho[x, 0] = jnp.concatenate([head[:16], head[16:]], axis=1).astype(BF)

    def slot(r):
        return jnp.where(r < 5, jnp.maximum(2 * r - 1, 0), 2 * NY - 2 * r)

    STEPS = (0, 1, 7, 2, 6, 3, 5, 4)
    for d in FAR_Y:
        k = STEPS.index(NY - d)
        send(ho.at[x, 0], ho.at[x, k], y_ss.at[d], y_rs.at[k], g, x * NY + ypeer(d))
    for k in range(1, 5):
        arrived(ho.at[x, k], y_rs.at[k])
    for d in FAR_X:
        piece = ho.at[x, 0:5]
        send(piece, piece, x_ss.at[0, d], x_rs.at[0, d], g, xpeer(d) * NY + y)
    for k in range(5, 8):
        arrived(ho.at[x, k], y_rs.at[k])
    for d in FAR_X:
        piece = ho.at[x, 5:8]
        send(piece, piece, x_ss.at[1, d], x_rs.at[1, d], g, xpeer(d) * NY + y)

    for e in (0, 1, 3, 2):
        xx = xpeer(e)
        if e:
            arrived(ho.at[xx, 0:5], x_rs.at[0, NX - e])
            arrived(ho.at[xx, 5:8], x_rs.at[1, NX - e])
        lhs = jnp.concatenate(
            [
                jnp.concatenate(
                    [ho[xx, slot((2 * tb + hp - y) % NY)] for hp in range(2)], axis=1
                )
                for tb in range(4)
            ],
            axis=0,
        )
        part = dot_nt(lhs, wo[...]).astype(BF)
        for tb in range(4):
            to = 4 * xx + tb
            zs[to] = part[tb * 16 : (tb + 1) * 16]

            @pl.when(to != g)
            def _():
                remote(zs.at[to], z_out.at[g], z_ss.at[to], z_rs.at[g], to, inner).start()

    own = pltpu.make_async_copy(zs.at[g], z_out.at[g], z_ss.at[g])
    own.start()
    for d in range(1, NG):
        arrived(z_out.at[gpeer(d)], z_rs.at[gpeer(d)])
    own.wait()
    for d in range(1, NG):
        remote(zs.at[gpeer(d)], z_out.at[g], z_ss.at[gpeer(d)], z_rs.at[g], g, inner).wait_send()
    for copy in sends:
        copy.wait_send()


def local(q, ids, limits, latent, ka, va, kd, ku, vd, vu, wo):
    args = (
        q, ids.reshape(1, -1), limits, latent.T, ka, va, kd.swapaxes(2, 3), ku,
        vd.swapaxes(2, 3), vu, wo.T,
    )
    sem = pltpu.SemaphoreType.DMA
    v = pltpu.VMEM
    parts = pl.pallas_call(
        kernel,
        out_shape=jax.ShapeDtypeStruct((NG, 16, 256), BF),
        in_specs=[pl.BlockSpec(memory_space=pltpu.HBM)] * len(args),
        out_specs=pl.BlockSpec(memory_space=pltpu.HBM),
        scratch_shapes=[
            v(q.shape, BF),
            v((TOK * HEADS, NOPE), F32),
            v((TOK * HEADS, NOPE), F32),
            v((1, ids.shape[0]), jnp.int32),
            pltpu.SMEM(limits.shape, jnp.int32),
            v((NX, LAT + ROPE, SPAN), BF),
            v(ka.shape, BF),
            v(va.shape, BF),
            v(args[6].shape, BF),
            v(ku.shape, BF),
            v(args[8].shape, BF),
            v(vu.shape, BF),
            v((256, LAT), BF),
            v((NY, 48, 128), BF),
            v((2, 2 * NY * TOK, LAT + 128), BF),
            v((NY, 48, 128), BF),
            v((NY, 48, 128), BF),
            v((NX, NY, 16, 256), BF),
            v((NG, 16, 256), BF),
            sem((len(args),)),
            *[sem((NY,))] * 2,
            *[sem((NX,))] * 4,
            *[sem((NY,))] * 4,
            *[sem((2, NX))] * 2,
            *[sem((NG,))] * 2,
        ],
        compiler_params=pltpu.CompilerParams(
            collective_id=0, has_side_effects=True
        ),
    )(*args)
    return jnp.sum(parts.astype(F32), axis=0)[:, : wo.shape[1]].astype(BF)


def solution(mesh):
    in_specs = (
        P("inner", "grp", None),
        P(),
        P(),
        P("inner", None),
        P("grp", None, None),
        P("grp", None, None),
        P(None, "grp", None, None),
        P(None, "grp", None, None),
        P(None, "grp", None, None),
        P(None, "grp", None, None),
        P("grp", "inner"),
    )
    return jax.shard_map(
        local, mesh=mesh, in_specs=in_specs, out_specs=P("grp", "inner"), check_vma=False
    )
```

```python
import functools

import jax
import jax.numpy as jnp
from jax import lax
from jax.experimental import pallas as pl
from jax.experimental.pallas import tpu as pltpu
from jax.sharding import PartitionSpec as P

MESH = pl.DeviceIdType.MESH
BF, F32 = jnp.bfloat16, jnp.float32
LAT, ROPE, NOPE = 512, 64, 128
NX, NY, NG = 4, 8, 16
HEADS, TOK = 4, 8
SPAN = 128
MASKED = -30000.0
FAR_Y, FAR_X = (4, 3, 5, 2, 6, 1, 7), (2, 1, 3)
SCALE = (NOPE + ROPE) ** -0.5


def dot(a, b):
    return lax.dot_general(a, b, (((1,), (0,)), ((), ())), preferred_element_type=F32)


def dot_nt(a, b):
    return lax.dot_general(a, b, (((1,), (1,)), ((), ())), preferred_element_type=F32)


def kernel(
    q_hbm, ids_hbm, lim_hbm, lat_hbm, ka_hbm, va_hbm, kd_hbm, ku_hbm, vd_hbm, vu_hbm, wo_hbm,
    z_out,
    q_v, q_n, q_r, ids_v, lim_s, lat, ka, va, kd, ku, vd, vu, wo,
    qbuf, qf, vs, rv, ho, zs,
    lsem, q_ss, q_rs, l_ss, l_rs, c_ss, c_rs, v_ss, v_rs, y_ss, y_rs, x_ss, x_rs, z_ss, z_rs, up_sem,
):
    g = lax.axis_index("grp")
    inner = lax.axis_index("inner")
    x, y = inner // NY, inner % NY
    z = g // 2
    core = 2 * z + 1 - g % 2

    def ypeer(d):
        return (y + d) % NY

    def xpeer(d):
        return (x + d) % NX

    def gpeer(d):
        return (g + d) % NG

    def remote(src, dst, ss, rs, to_g, to_inner):
        return pltpu.make_async_remote_copy(
            src_ref=src, dst_ref=dst, send_sem=ss, recv_sem=rs,
            device_id=(to_g, to_inner), device_id_type=MESH,
        )

    def load(n, src, dst):
        copy = pltpu.make_async_copy(src, dst, lsem.at[n])
        copy.start()
        return copy

    def arrived(dst, rs):
        remote(dst, dst, q_ss.at[0], rs, g, inner).wait_recv()

    sends = []

    def send(*what):
        copy = remote(*what)
        copy.start()
        sends.append(copy)

    get_q = load(0, q_hbm, q_v)
    get_lat = load(1, lat_hbm, lat.at[x])
    barrier = pltpu.get_barrier_semaphore()
    for d in FAR_Y:
        pl.semaphore_signal(barrier, 1, device_id=(g, x * NY + ypeer(d)), device_id_type=MESH)
    for d in FAR_X:
        pl.semaphore_signal(barrier, 1, device_id=(g, xpeer(d) * NY + y), device_id_type=MESH)
    pl.semaphore_signal(barrier, 1, device_id=(core, inner), device_id_type=MESH)
    for k in range(NG):

        @pl.when(k // 2 > z)
        def _():
            pl.semaphore_signal(barrier, 1, device_id=(k, inner), device_id_type=MESH)

    pl.semaphore_wait(barrier, NY - 1 + NX - 1 + 1 + 2 * z)
    part = pl.ds(pl.multiple_of((g % 2) * 288, 16), 288)
    for d in FAR_X:
        send(lat_hbm.at[part], lat.at[x, part], l_ss.at[d], l_rs.at[x], g, xpeer(d) * NY + y)

    get_q.wait()
    q32 = q_v[...].astype(F32)
    for t in range(TOK):
        q_n[t * HEADS : (t + 1) * HEADS, :] = q32[t, :, :NOPE]
        q_r[t * HEADS : (t + 1) * HEADS, :ROPE] = q32[t, :, NOPE:]
    rows = [q_n[pl.ds(h, TOK, stride=HEADS), :] for h in range(HEADS)]
    ropes = [q_r[pl.ds(h, TOK, stride=HEADS), :][:, :ROPE] for h in range(HEADS)]
    rows += [jnp.concatenate(ropes[h : h + 2], axis=1) for h in (0, 2)]
    qbuf[y] = jnp.concatenate(rows, axis=0).astype(BF)
    for d in FAR_Y:
        send(qbuf.at[y], qbuf.at[y], q_ss.at[d], q_rs.at[y], g, x * NY + ypeer(d))
    for k in range(NG):

        @pl.when(k // 2 < z)
        def _():
            pl.semaphore_signal(up_sem, 1, device_id=(k, inner), device_id_type=MESH)

    get = [
        load(n + 2, src, dst)
        for n, (src, dst) in enumerate((
            (ids_hbm, ids_v), (lim_hbm, lim_s), (ka_hbm, ka), (kd_hbm, kd), (ku_hbm, ku), (va_hbm, va),
            (vd_hbm, vd), (vu_hbm, vu), (wo_hbm, wo.at[: wo_hbm.shape[0]]),
        ))
    ]

    wo[wo_hbm.shape[0] :, :] = jnp.zeros((wo.shape[0] - wo_hbm.shape[0], LAT), BF)
    for copy in [get_lat] + get:
        copy.wait()
    span = NY * TOK
    wide = NX * span
    row = lax.broadcasted_iota(jnp.int32, (span, wide), 0)
    lane = lax.broadcasted_iota(jnp.int32, (span, wide), 1)
    tenant = jnp.sum(jnp.where(lane == row + x * span, ids_v[...], 0), axis=1, keepdims=True)
    limit = jnp.zeros_like(tenant)
    for k in range(4):
        limit = jnp.where(tenant == k, lim_s[k], limit)
    chosen = lax.broadcasted_iota(jnp.int32, (span, 64), 1) // 16 == tenant

    for d in FAR_Y:
        arrived(qbuf.at[ypeer(d)], q_rs.at[ypeer(d)])
    for d in (1, 3, 2):
        piece = lat.at[xpeer(d), part]
        arrived(piece, l_rs.at[xpeer(d)])
        send(piece, piece, c_ss.at[d], c_rs.at[d], core, inner)

    blocks = [qbuf[k].astype(F32) for k in range(NY)]
    half = lax.broadcasted_iota(jnp.int32, (span, NOPE), 1) // ROPE
    for h in range(HEADS):
        nope = jnp.concatenate([b[h * TOK : (h + 1) * TOK] for b in blocks], axis=0).astype(BF)
        first = HEADS * TOK + (h // 2) * TOK
        rope = jnp.concatenate([b[first : first + TOK] for b in blocks], axis=0)
        low = dot_nt(nope, kd[:, h].reshape(64, NOPE))
        low = jnp.where(chosen, low, 0.0).astype(BF)
        latent = dot(nope, ka[h]) + dot(low, ku[:, h].reshape(64, LAT))
        rows = pl.ds((h % 2) * span, span)
        qf[h // 2, rows, :LAT] = latent.astype(BF)
        qf[h // 2, rows, LAT:] = jnp.where(half == h % 2, rope, 0.0).astype(BF)

    other = pl.ds(pl.multiple_of((1 - g % 2) * 288, 16), 288)
    for d in (1, 3, 2):
        arrived(lat.at[xpeer(d), other], c_rs.at[d])

    base = lax.broadcasted_iota(jnp.int32, (2 * span, SPAN), 1) + y * SPAN
    limit2 = jnp.concatenate([limit, limit], axis=0)
    eye = lax.broadcasted_iota(jnp.int32, (SPAN, SPAN), 0) == lax.broadcasted_iota(
        jnp.int32, (SPAN, SPAN), 1
    )
    okay = [base + b * NY * SPAN < limit2 for b in range(NX)]
    for turn, peers in enumerate(((4, 2, 6, 0), (3, 5, 1, 7))):
        hp = (y + turn) % 2
        mine = qf[hp]
        scores = []
        for b in range(NX):
            keys = jnp.concatenate([lat[b], lat[b, LAT:]], axis=0)
            scores.append(jnp.where(okay[b], dot(mine, keys) * SCALE, MASKED))
        top = functools.reduce(jnp.maximum, scores)
        top = jnp.max(top, axis=1, keepdims=True)
        weights = [jnp.where(ok, jnp.exp(s - top), 0.0) for ok, s in zip(okay, scores)]
        total = jnp.sum(functools.reduce(jnp.add, weights), axis=1, keepdims=True)
        acc = functools.reduce(
            jnp.add, [dot_nt(w.astype(BF), lat[b, :LAT]) for b, w in enumerate(weights)]
        ).astype(BF)
        three = []
        for column in (top, total):
            rest = jnp.sum(jnp.where(eye, column, 0.0), axis=0, keepdims=True)
            for _ in range(3):
                three.append(rest.astype(BF).astype(F32))
                rest = rest - three[-1]
        three = jnp.concatenate(three + [jnp.zeros((10, SPAN), F32)], axis=0).astype(BF)
        values = []
        for hl in range(2):
            h = hp * 2 + hl
            mine = acc[hl * span : (hl + 1) * span, :]
            low = dot_nt(mine, vd[:, h].reshape(64, LAT))
            low = jnp.where(chosen, low, 0.0).astype(BF)
            values.append((dot(mine, va[h]) + dot(low, vu[:, h].reshape(64, NOPE))).astype(BF))
        for tb in range(4):
            vs[tb * 2 + hp] = jnp.concatenate(
                [values[0][tb * 16 : (tb + 1) * 16], values[1][tb * 16 : (tb + 1) * 16], three], axis=0
            )
        for d in peers:
            if d:
                to = ypeer(d)
                send(vs.at[to], rv.at[NY - d], v_ss.at[d], v_rs.at[NY - d], g, x * NY + to)
            else:
                rv[0] = vs[y]

    r32 = lax.broadcasted_iota(jnp.int32, (32, SPAN), 0)
    l32 = lax.broadcasted_iota(jnp.int32, (32, SPAN), 1)
    pick = l32 == (r32 // 16) * span + (y // 2) * 16 + r32 % 16
    for d in (2, 6, 4, 1, 7, 3, 5):
        arrived(rv.at[d], v_rs.at[d])
    tops, totals = [], []
    for k in range(NY):
        three = rv[k, 32:48, :].astype(F32)
        tops.append(three[0:1] + three[1:2] + three[2:3])
        totals.append(three[3:4] + three[4:5] + three[5:6])
    peak = functools.reduce(jnp.maximum, tops)
    factors = [jnp.exp(t - peak) for t in tops]
    denom = functools.reduce(jnp.add, [f * t for f, t in zip(factors, totals)])
    shares = [
        jnp.sum(jnp.where(pick, f / denom, 0.0), axis=1, keepdims=True) for f in factors
    ]
    head = functools.reduce(
        jnp.add, [s * rv[k, :32, :].astype(F32) for k, s in enumerate(shares)]
    )
    ho[x, 0] = jnp.concatenate([head[:16], head[16:]], axis=1).astype(BF)

    def slot(r):
        return jnp.where(r < 5, jnp.maximum(2 * r - 1, 0), 2 * NY - 2 * r)

    STEPS = (0, 1, 7, 2, 6, 3, 5, 4)
    for d in FAR_Y:
        k = STEPS.index(NY - d)
        send(ho.at[x, 0], ho.at[x, k], y_ss.at[d], y_rs.at[k], g, x * NY + ypeer(d))
    for k in range(1, 5):
        arrived(ho.at[x, k], y_rs.at[k])
    for d in FAR_X:
        piece = ho.at[x, 0:5]
        send(piece, piece, x_ss.at[0, d], x_rs.at[0, x], g, xpeer(d) * NY + y)
    for k in range(5, 8):
        arrived(ho.at[x, k], y_rs.at[k])
    for d in FAR_X:
        piece = ho.at[x, 5:8]
        send(piece, piece, x_ss.at[1, d], x_rs.at[1, x], g, xpeer(d) * NY + y)

    @pl.when(z < NG // 2 - 1)
    def _():
        pl.semaphore_wait(up_sem, NG - 2 - 2 * z)

    for xx in range(NX):

        @pl.when(xx != x)
        def _():
            arrived(ho.at[xx, 0:5], x_rs.at[0, xx])
            arrived(ho.at[xx, 5:8], x_rs.at[1, xx])

        lhs = jnp.concatenate(
            [
                jnp.concatenate(
                    [ho[xx, slot((2 * tb + hp - y) % NY)] for hp in range(2)], axis=1
                )
                for tb in range(4)
            ],
            axis=0,
        )
        part = dot_nt(lhs, wo[...]).astype(BF)
        for tb in range(4):
            to = 4 * xx + tb
            zs[to] = part[tb * 16 : (tb + 1) * 16]

            @pl.when(to != g)
            def _():
                remote(zs.at[to], z_out.at[g], z_ss.at[to], z_rs.at[g], to, inner).start()

    own = pltpu.make_async_copy(zs.at[g], z_out.at[g], z_ss.at[g])
    own.start()
    for d in range(1, NG):
        arrived(z_out.at[gpeer(d)], z_rs.at[gpeer(d)])
    own.wait()
    for d in range(1, NG):
        remote(zs.at[gpeer(d)], z_out.at[g], z_ss.at[gpeer(d)], z_rs.at[g], g, inner).wait_send()
    for copy in sends:
        copy.wait_send()


def local(q, ids, limits, latent, ka, va, kd, ku, vd, vu, wo):
    args = (
        q, ids.reshape(1, -1), limits, latent.T, ka, va, kd.swapaxes(2, 3), ku,
        vd.swapaxes(2, 3), vu, wo.T,
    )
    sem = pltpu.SemaphoreType.DMA
    v = pltpu.VMEM
    parts = pl.pallas_call(
        kernel,
        out_shape=pltpu.VMEM((NG, 16, 256), BF),
        in_specs=[pl.BlockSpec(memory_space=pltpu.HBM)] * len(args),
        out_specs=pl.BlockSpec(memory_space=pltpu.VMEM),
        scratch_shapes=[
            v(q.shape, BF),
            v((TOK * HEADS, NOPE), F32),
            v((TOK * HEADS, NOPE), F32),
            v((1, ids.shape[0]), jnp.int32),
            pltpu.SMEM(limits.shape, jnp.int32),
            v((NX, LAT + ROPE, SPAN), BF),
            v(ka.shape, BF),
            v(va.shape, BF),
            v(args[6].shape, BF),
            v(ku.shape, BF),
            v(args[8].shape, BF),
            v(vu.shape, BF),
            v((256, LAT), BF),
            v((NY, 48, 128), BF),
            v((2, 2 * NY * TOK, LAT + 128), BF),
            v((NY, 48, 128), BF),
            v((NY, 48, 128), BF),
            v((NX, NY, 16, 256), BF),
            v((NG, 16, 256), BF),
            sem((len(args),)),
            *[sem((NY,))] * 2,
            *[sem((NX,))] * 4,
            *[sem((NY,))] * 4,
            *[sem((2, NX))] * 2,
            *[sem((NG,))] * 2,
            pltpu.SemaphoreType.REGULAR,
        ],
        compiler_params=pltpu.CompilerParams(
            collective_id=0, has_side_effects=True
        ),
    )(*args)
    return jnp.sum(parts.astype(F32), axis=0)[:, : wo.shape[1]].astype(BF)


def solution(mesh):
    in_specs = (
        P("inner", "grp", None),
        P(),
        P(),
        P("inner", None),
        P("grp", None, None),
        P("grp", None, None),
        P(None, "grp", None, None),
        P(None, "grp", None, None),
        P(None, "grp", None, None),
        P(None, "grp", None, None),
        P("grp", "inner"),
    )
    return jax.shard_map(
        local, mesh=mesh, in_specs=in_specs, out_specs=P("grp", "inner"), check_vma=False
    )
```

```python
import functools

import jax
import jax.numpy as jnp
from jax import lax
from jax.experimental import pallas as pl
from jax.experimental.pallas import tpu as pltpu
from jax.sharding import PartitionSpec as P

MESH = pl.DeviceIdType.MESH
BF, F32 = jnp.bfloat16, jnp.float32
LAT, ROPE, NOPE = 512, 64, 128
NX, NY, NG = 4, 8, 16
HEADS, TOK = 4, 8
SPAN = 128
MASKED = -30000.0
FAR_Y, FAR_X = (4, 3, 5, 2, 6, 1, 7), (2, 1, 3)
SCALE = (NOPE + ROPE) ** -0.5


def dot(a, b):
    return lax.dot_general(a, b, (((1,), (0,)), ((), ())), preferred_element_type=F32)


def dot_nt(a, b):
    return lax.dot_general(a, b, (((1,), (1,)), ((), ())), preferred_element_type=F32)


def kernel(
    q_hbm, ids_hbm, lim_hbm, lat_hbm, ka_hbm, va_hbm, kd_hbm, ku_hbm, vd_hbm, vu_hbm, wo_hbm,
    z_out,
    q_v, q_n, q_r, ids_v, lim_s, lat, ka, va, kd, ku, vd, vu, wo,
    qbuf, qf, vs, rv, ho, zs,
    lsem, q_ss, q_rs, l_ss, l_rs, c_ss, c_rs, v_ss, v_rs, y_ss, y_rs, x_ss, x_rs, z_ss, z_rs, up_sem,
):
    g = lax.axis_index("grp")
    inner = lax.axis_index("inner")
    x, y = inner // NY, inner % NY
    z = g // 2
    core = 2 * z + 1 - g % 2

    def ypeer(d):
        return (y + d) % NY

    def xpeer(d):
        return (x + d) % NX

    def gpeer(d):
        return (g + d) % NG

    def remote(src, dst, ss, rs, to_g, to_inner):
        return pltpu.make_async_remote_copy(
            src_ref=src, dst_ref=dst, send_sem=ss, recv_sem=rs,
            device_id=(to_g, to_inner), device_id_type=MESH,
        )

    def load(n, src, dst):
        copy = pltpu.make_async_copy(src, dst, lsem.at[n])
        copy.start()
        return copy

    def arrived(dst, rs):
        remote(dst, dst, q_ss, rs, g, inner).wait_recv()

    def send(*what):
        remote(*what).start()

    get_q = load(0, q_hbm, q_v)
    get_lat = load(1, lat_hbm, lat.at[x])
    barrier = pltpu.get_barrier_semaphore()
    for d in FAR_Y:
        pl.semaphore_signal(barrier, 1, device_id=(g, x * NY + ypeer(d)), device_id_type=MESH)
    for d in FAR_X:
        pl.semaphore_signal(barrier, 1, device_id=(g, xpeer(d) * NY + y), device_id_type=MESH)
    pl.semaphore_signal(barrier, 1, device_id=(core, inner), device_id_type=MESH)
    for k in range(NG):

        @pl.when(k // 2 > z)
        def _():
            pl.semaphore_signal(barrier, 1, device_id=(k, inner), device_id_type=MESH)

    pl.semaphore_wait(barrier, NY - 1 + NX - 1 + 1 + 2 * z)
    part = pl.ds(pl.multiple_of((g % 2) * 288, 16), 288)
    for d in FAR_X:
        send(lat_hbm.at[part], lat.at[x, part], l_ss, l_rs.at[x], g, xpeer(d) * NY + y)

    get_q.wait()
    q32 = q_v[...].astype(F32)
    for t in range(TOK):
        q_n[t * HEADS : (t + 1) * HEADS, :] = q32[t, :, :NOPE]
        q_r[t * HEADS : (t + 1) * HEADS, :ROPE] = q32[t, :, NOPE:]
    rows = [q_n[pl.ds(h, TOK, stride=HEADS), :] for h in range(HEADS)]
    ropes = [q_r[pl.ds(h, TOK, stride=HEADS), :][:, :ROPE] for h in range(HEADS)]
    rows += [jnp.concatenate(ropes[h : h + 2], axis=1) for h in (0, 2)]
    qbuf[y] = jnp.concatenate(rows, axis=0).astype(BF)
    for d in FAR_Y:
        send(qbuf.at[y], qbuf.at[y], q_ss, q_rs, g, x * NY + ypeer(d))
    for k in range(NG):

        @pl.when(k // 2 < z)
        def _():
            pl.semaphore_signal(up_sem, 1, device_id=(k, inner), device_id_type=MESH)

    get = [
        load(n + 2, src, dst)
        for n, (src, dst) in enumerate((
            (ids_hbm, ids_v), (lim_hbm, lim_s), (ka_hbm, ka), (kd_hbm, kd), (ku_hbm, ku), (va_hbm, va),
            (vd_hbm, vd), (vu_hbm, vu), (wo_hbm, wo.at[: wo_hbm.shape[0]]),
        ))
    ]

    wo[wo_hbm.shape[0] :, :] = jnp.zeros((wo.shape[0] - wo_hbm.shape[0], LAT), BF)
    for copy in [get_lat] + get:
        copy.wait()
    span = NY * TOK
    wide = NX * span
    row = lax.broadcasted_iota(jnp.int32, (span, wide), 0)
    lane = lax.broadcasted_iota(jnp.int32, (span, wide), 1)
    tenant = jnp.sum(jnp.where(lane == row + x * span, ids_v[...], 0), axis=1, keepdims=True)
    limit = jnp.zeros_like(tenant)
    for k in range(4):
        limit = jnp.where(tenant == k, lim_s[k], limit)
    chosen = lax.broadcasted_iota(jnp.int32, (span, 64), 1) // 16 == tenant

    arrived(qbuf.at[: NY - 1], q_rs)
    for d in (1, 3, 2):
        piece = lat.at[xpeer(d), part]
        arrived(piece, l_rs.at[xpeer(d)])
        send(piece, piece, c_ss, c_rs, core, inner)

    blocks = [qbuf[k].astype(F32) for k in range(NY)]
    half = lax.broadcasted_iota(jnp.int32, (span, NOPE), 1) // ROPE
    for h in range(HEADS):
        nope = jnp.concatenate([b[h * TOK : (h + 1) * TOK] for b in blocks], axis=0).astype(BF)
        first = HEADS * TOK + (h // 2) * TOK
        rope = jnp.concatenate([b[first : first + TOK] for b in blocks], axis=0)
        low = dot_nt(nope, kd[:, h].reshape(64, NOPE))
        low = jnp.where(chosen, low, 0.0).astype(BF)
        latent = dot(nope, ka[h]) + dot(low, ku[:, h].reshape(64, LAT))
        rows = pl.ds((h % 2) * span, span)
        qf[h // 2, rows, :LAT] = latent.astype(BF)
        qf[h // 2, rows, LAT:] = jnp.where(half == h % 2, rope, 0.0).astype(BF)

    other = pl.ds(pl.multiple_of((1 - g % 2) * 288, 16), 288)
    arrived(lat.at[: NX - 1, other], c_rs)

    base = lax.broadcasted_iota(jnp.int32, (2 * span, SPAN), 1) + y * SPAN
    limit2 = jnp.concatenate([limit, limit], axis=0)
    eye = lax.broadcasted_iota(jnp.int32, (SPAN, SPAN), 0) == lax.broadcasted_iota(
        jnp.int32, (SPAN, SPAN), 1
    )
    okay = [base + b * NY * SPAN < limit2 for b in range(NX)]
    for turn, peers in enumerate(((4, 2, 6, 0), (3, 5, 1, 7))):
        hp = (y + turn) % 2
        mine = qf[hp]
        scores = []
        for b in range(NX):
            keys = jnp.concatenate([lat[b], lat[b, LAT:]], axis=0)
            scores.append(jnp.where(okay[b], dot(mine, keys) * SCALE, MASKED))
        top = functools.reduce(jnp.maximum, scores)
        top = jnp.max(top, axis=1, keepdims=True)
        weights = [jnp.where(ok, jnp.exp(s - top), 0.0) for ok, s in zip(okay, scores)]
        total = jnp.sum(functools.reduce(jnp.add, weights), axis=1, keepdims=True)
        acc = functools.reduce(
            jnp.add, [dot_nt(w.astype(BF), lat[b, :LAT]) for b, w in enumerate(weights)]
        ).astype(BF)
        three = []
        for column in (top, total):
            rest = jnp.sum(jnp.where(eye, column, 0.0), axis=0, keepdims=True)
            for _ in range(3):
                three.append(rest.astype(BF).astype(F32))
                rest = rest - three[-1]
        three = jnp.concatenate(three + [jnp.zeros((10, SPAN), F32)], axis=0).astype(BF)
        values = []
        for hl in range(2):
            h = hp * 2 + hl
            mine = acc[hl * span : (hl + 1) * span, :]
            low = dot_nt(mine, vd[:, h].reshape(64, LAT))
            low = jnp.where(chosen, low, 0.0).astype(BF)
            values.append((dot(mine, va[h]) + dot(low, vu[:, h].reshape(64, NOPE))).astype(BF))
        for tb in range(4):
            vs[tb * 2 + hp] = jnp.concatenate(
                [values[0][tb * 16 : (tb + 1) * 16], values[1][tb * 16 : (tb + 1) * 16], three], axis=0
            )
        for d in peers:
            if d:
                to = ypeer(d)
                send(vs.at[to], rv.at[NY - d], v_ss, v_rs, g, x * NY + to)
            else:
                rv[0] = vs[y]

    r32 = lax.broadcasted_iota(jnp.int32, (32, SPAN), 0)
    l32 = lax.broadcasted_iota(jnp.int32, (32, SPAN), 1)
    pick = l32 == (r32 // 16) * span + (y // 2) * 16 + r32 % 16
    arrived(rv.at[: NY - 1], v_rs)
    tops, totals = [], []
    for k in range(NY):
        three = rv[k, 32:48, :].astype(F32)
        tops.append(three[0:1] + three[1:2] + three[2:3])
        totals.append(three[3:4] + three[4:5] + three[5:6])
    peak = functools.reduce(jnp.maximum, tops)
    factors = [jnp.exp(t - peak) for t in tops]
    denom = functools.reduce(jnp.add, [f * t for f, t in zip(factors, totals)])
    shares = [
        jnp.sum(jnp.where(pick, f / denom, 0.0), axis=1, keepdims=True) for f in factors
    ]
    head = functools.reduce(
        jnp.add, [s * rv[k, :32, :].astype(F32) for k, s in enumerate(shares)]
    )
    ho[x, 0] = jnp.concatenate([head[:16], head[16:]], axis=1).astype(BF)

    def slot(r):
        return jnp.where(r < 5, jnp.maximum(2 * r - 1, 0), 2 * NY - 2 * r)

    STEPS = (0, 1, 7, 2, 6, 3, 5, 4)
    for d in FAR_Y:
        k = STEPS.index(NY - d)
        send(ho.at[x, 0], ho.at[x, k], y_ss, y_rs.at[k // 5], g, x * NY + ypeer(d))
    arrived(ho.at[x, 1:5], y_rs.at[0])
    for d in FAR_X:
        piece = ho.at[x, 0:5]
        send(piece, piece, x_ss, x_rs.at[x], g, xpeer(d) * NY + y)
    arrived(ho.at[x, 5:8], y_rs.at[1])
    for d in FAR_X:
        piece = ho.at[x, 5:8]
        send(piece, piece, x_ss, x_rs.at[x], g, xpeer(d) * NY + y)

    @pl.when(z < NG // 2 - 1)
    def _():
        pl.semaphore_wait(up_sem, NG - 2 - 2 * z)

    for xx in range(NX):

        @pl.when(xx != x)
        def _():
            arrived(ho.at[xx], x_rs.at[xx])

        lhs = jnp.concatenate(
            [
                jnp.concatenate(
                    [ho[xx, slot((2 * tb + hp - y) % NY)] for hp in range(2)], axis=1
                )
                for tb in range(4)
            ],
            axis=0,
        )
        share = dot_nt(lhs, wo[...]).astype(BF)
        for tb in range(4):
            to = 4 * xx + tb
            zs[to] = share[tb * 16 : (tb + 1) * 16]

            @pl.when(to != g)
            def _():
                remote(zs.at[to], z_out.at[g], z_ss, z_rs, to, inner).start()

    z_out[g] = zs[g]
    arrived(z_out.at[: NG - 1], z_rs)
    for sent, sem in (
        (qbuf.at[: NY - 1], q_ss), (lat.at[: NX - 1, part], l_ss), (lat.at[: NX - 1, part], c_ss),
        (rv.at[: NY - 1], v_ss), (ho.at[0, : NY - 1], y_ss), (ho.at[: NX - 1], x_ss),
        (zs.at[: NG - 1], z_ss),
    ):
        remote(sent, sent, sem, q_rs, g, inner).wait_send()


def local(q, ids, limits, latent, ka, va, kd, ku, vd, vu, wo):
    args = (
        q, ids.reshape(1, -1), limits, latent.T, ka, va, kd.swapaxes(2, 3), ku,
        vd.swapaxes(2, 3), vu, wo.T,
    )
    sem = pltpu.SemaphoreType.DMA
    v = pltpu.VMEM
    parts = pl.pallas_call(
        kernel,
        out_shape=pltpu.VMEM((NG, 16, 256), BF),
        in_specs=[pl.BlockSpec(memory_space=pltpu.HBM)] * len(args),
        out_specs=pl.BlockSpec(memory_space=pltpu.VMEM),
        scratch_shapes=[
            v(q.shape, BF),
            v((TOK * HEADS, NOPE), F32),
            v((TOK * HEADS, NOPE), F32),
            v((1, ids.shape[0]), jnp.int32),
            pltpu.SMEM(limits.shape, jnp.int32),
            v((NX, LAT + ROPE, SPAN), BF),
            v(ka.shape, BF),
            v(va.shape, BF),
            v(args[6].shape, BF),
            v(ku.shape, BF),
            v(args[8].shape, BF),
            v(vu.shape, BF),
            v((256, LAT), BF),
            v((NY, 48, 128), BF),
            v((2, 2 * NY * TOK, LAT + 128), BF),
            v((NY, 48, 128), BF),
            v((NY, 48, 128), BF),
            v((NX, NY, 16, 256), BF),
            v((NG, 16, 256), BF),
            sem((len(args),)),
            *[sem] * 3,
            sem((NX,)),
            *[sem] * 5,
            sem((2,)),
            sem,
            sem((NX,)),
            *[sem] * 2,
            pltpu.SemaphoreType.REGULAR,
        ],
        compiler_params=pltpu.CompilerParams(
            collective_id=0, has_side_effects=True
        ),
    )(*args)
    return jnp.sum(parts.astype(F32), axis=0)[:, : wo.shape[1]].astype(BF)


def solution(mesh):
    in_specs = (
        P("inner", "grp", None),
        P(),
        P(),
        P("inner", None),
        P("grp", None, None),
        P("grp", None, None),
        P(None, "grp", None, None),
        P(None, "grp", None, None),
        P(None, "grp", None, None),
        P(None, "grp", None, None),
        P("grp", "inner"),
    )
    return jax.shard_map(
        local, mesh=mesh, in_specs=in_specs, out_specs=P("grp", "inner"), check_vma=False
    )
```

```python
import functools

import jax
import jax.numpy as jnp
from jax import lax
from jax.experimental import pallas as pl
from jax.experimental.pallas import tpu as pltpu
from jax.sharding import PartitionSpec as P

MESH = pl.DeviceIdType.MESH
BF, F32 = jnp.bfloat16, jnp.float32
LAT, ROPE, NOPE = 512, 64, 128
NX, NY, NG = 4, 8, 16
HEADS, TOK = 4, 8
SPAN = 128
MASKED = -30000.0
FAR_Y, FAR_X = (4, 3, 5, 2, 6, 1, 7), (2, 1, 3)
SCALE = (NOPE + ROPE) ** -0.5


def dot(a, b):
    return lax.dot_general(a, b, (((1,), (0,)), ((), ())), preferred_element_type=F32)


def dot_nt(a, b):
    return lax.dot_general(a, b, (((1,), (1,)), ((), ())), preferred_element_type=F32)


def kernel(
    q_hbm, ids_hbm, lim_hbm, lat_hbm, ka_hbm, va_hbm, kd_hbm, ku_hbm, vd_hbm, vu_hbm, wo_hbm,
    z_out,
    q_v, q_n, q_r, ids_v, lim_s, lat, ka, va, kd, ku, vd, vu, wo,
    qbuf, qf, vs, rv, ho, zs,
    lsem, q_ss, q_rs, l_ss, l_rs, c_ss, c_rs, v_ss, v_rs, y_ss, y_rs, x_ss, x_rs, z_ss, z_rs, up_sem,
):
    g = lax.axis_index("grp")
    inner = lax.axis_index("inner")
    x, y = inner // NY, inner % NY
    z = g // 2
    core = 2 * z + 1 - g % 2

    def ypeer(d):
        return (y + d) % NY

    def xpeer(d):
        return (x + d) % NX

    def gpeer(d):
        return (g + d) % NG

    def remote(src, dst, ss, rs, to_g, to_inner):
        return pltpu.make_async_remote_copy(
            src_ref=src, dst_ref=dst, send_sem=ss, recv_sem=rs,
            device_id=(to_g, to_inner), device_id_type=MESH,
        )

    def load(n, src, dst):
        copy = pltpu.make_async_copy(src, dst, lsem.at[n])
        copy.start()
        return copy

    def arrived(dst, rs):
        remote(dst, dst, q_ss, rs, g, inner).wait_recv()

    def send(*what):
        remote(*what).start()

    get_q = load(0, q_hbm, q_v)
    get_lat = load(1, lat_hbm, lat.at[x])
    barrier = pltpu.get_barrier_semaphore()
    for d in FAR_Y:
        pl.semaphore_signal(barrier, 1, device_id=(g, x * NY + ypeer(d)), device_id_type=MESH)
    for d in FAR_X:
        pl.semaphore_signal(barrier, 1, device_id=(g, xpeer(d) * NY + y), device_id_type=MESH)
    pl.semaphore_signal(barrier, 1, device_id=(core, inner), device_id_type=MESH)
    @pl.loop(2 * z + 2, NG)
    def _(k):
        pl.semaphore_signal(barrier, 1, device_id=(k, inner), device_id_type=MESH)

    pl.semaphore_wait(barrier, NY - 1 + NX - 1 + 1 + 2 * z)
    part = pl.ds(pl.multiple_of((g % 2) * 288, 16), 288)
    for d in FAR_X:
        send(lat_hbm.at[part], lat.at[x, part], l_ss, l_rs.at[x], g, xpeer(d) * NY + y)

    get_q.wait()
    q32 = q_v[...].astype(F32)
    for t in range(TOK):
        q_n[t * HEADS : (t + 1) * HEADS, :] = q32[t, :, :NOPE]
        q_r[t * HEADS : (t + 1) * HEADS, :ROPE] = q32[t, :, NOPE:]
    rows = [q_n[pl.ds(h, TOK, stride=HEADS), :] for h in range(HEADS)]
    ropes = [q_r[pl.ds(h, TOK, stride=HEADS), :][:, :ROPE] for h in range(HEADS)]
    rows += [jnp.concatenate(ropes[h : h + 2], axis=1) for h in (0, 2)]
    qbuf[y] = jnp.concatenate(rows, axis=0).astype(BF)
    for d in FAR_Y:
        send(qbuf.at[y], qbuf.at[y], q_ss, q_rs, g, x * NY + ypeer(d))
    @pl.loop(0, 2 * z)
    def _(k):
        pl.semaphore_signal(up_sem, 1, device_id=(k, inner), device_id_type=MESH)

    get = [
        load(n + 2, src, dst)
        for n, (src, dst) in enumerate((
            (ids_hbm, ids_v), (lim_hbm, lim_s), (ka_hbm, ka), (kd_hbm, kd), (ku_hbm, ku), (va_hbm, va),
            (vd_hbm, vd), (vu_hbm, vu), (wo_hbm, wo.at[: wo_hbm.shape[0]]),
        ))
    ]

    wo[wo_hbm.shape[0] :, :] = jnp.zeros((wo.shape[0] - wo_hbm.shape[0], LAT), BF)
    for copy in [get_lat] + get:
        copy.wait()
    span = NY * TOK
    wide = NX * span
    row = lax.broadcasted_iota(jnp.int32, (span, wide), 0)
    lane = lax.broadcasted_iota(jnp.int32, (span, wide), 1)
    tenant = jnp.sum(jnp.where(lane == row + x * span, ids_v[...], 0), axis=1, keepdims=True)
    limit = jnp.zeros_like(tenant)
    for k in range(4):
        limit = jnp.where(tenant == k, lim_s[k], limit)
    chosen = lax.broadcasted_iota(jnp.int32, (span, 64), 1) // 16 == tenant

    arrived(qbuf.at[: NY - 1], q_rs)
    for d in (1, 3, 2):
        piece = lat.at[xpeer(d), part]
        arrived(piece, l_rs.at[xpeer(d)])
        send(piece, piece, c_ss, c_rs, core, inner)

    blocks = [qbuf[k].astype(F32) for k in range(NY)]
    half = lax.broadcasted_iota(jnp.int32, (span, NOPE), 1) // ROPE
    for h in range(HEADS):
        nope = jnp.concatenate([b[h * TOK : (h + 1) * TOK] for b in blocks], axis=0).astype(BF)
        first = HEADS * TOK + (h // 2) * TOK
        rope = jnp.concatenate([b[first : first + TOK] for b in blocks], axis=0)
        low = dot_nt(nope, kd[:, h].reshape(64, NOPE))
        low = jnp.where(chosen, low, 0.0).astype(BF)
        latent = dot(nope, ka[h]) + dot(low, ku[:, h].reshape(64, LAT))
        rows = pl.ds((h % 2) * span, span)
        qf[h // 2, rows, :LAT] = latent.astype(BF)
        qf[h // 2, rows, LAT:] = jnp.where(half == h % 2, rope, 0.0).astype(BF)

    other = pl.ds(pl.multiple_of((1 - g % 2) * 288, 16), 288)
    arrived(lat.at[: NX - 1, other], c_rs)

    base = lax.broadcasted_iota(jnp.int32, (2 * span, SPAN), 1) + y * SPAN
    limit2 = jnp.concatenate([limit, limit], axis=0)
    eye = lax.broadcasted_iota(jnp.int32, (SPAN, SPAN), 0) == lax.broadcasted_iota(
        jnp.int32, (SPAN, SPAN), 1
    )
    okay = [base + b * NY * SPAN < limit2 for b in range(NX)]
    for turn, peers in enumerate(((4, 2, 6, 0), (3, 5, 1, 7))):
        hp = (y + turn) % 2
        mine = qf[hp]
        scores = []
        for b in range(NX):
            keys = jnp.concatenate([lat[b], lat[b, LAT:]], axis=0)
            scores.append(jnp.where(okay[b], dot(mine, keys) * SCALE, MASKED))
        top = functools.reduce(jnp.maximum, scores)
        top = jnp.max(top, axis=1, keepdims=True)
        weights = [jnp.where(ok, jnp.exp(s - top), 0.0) for ok, s in zip(okay, scores)]
        total = jnp.sum(functools.reduce(jnp.add, weights), axis=1, keepdims=True)
        acc = functools.reduce(
            jnp.add, [dot_nt(w.astype(BF), lat[b, :LAT]) for b, w in enumerate(weights)]
        ).astype(BF)
        three = []
        for column in (top, total):
            rest = jnp.sum(jnp.where(eye, column, 0.0), axis=0, keepdims=True)
            for _ in range(3):
                three.append(rest.astype(BF).astype(F32))
                rest = rest - three[-1]
        three = jnp.concatenate(three + [jnp.zeros((10, SPAN), F32)], axis=0).astype(BF)
        values = []
        for hl in range(2):
            h = hp * 2 + hl
            mine = acc[hl * span : (hl + 1) * span, :]
            low = dot_nt(mine, vd[:, h].reshape(64, LAT))
            low = jnp.where(chosen, low, 0.0).astype(BF)
            values.append((dot(mine, va[h]) + dot(low, vu[:, h].reshape(64, NOPE))).astype(BF))
        for tb in range(4):
            vs[tb * 2 + hp] = jnp.concatenate(
                [values[0][tb * 16 : (tb + 1) * 16], values[1][tb * 16 : (tb + 1) * 16], three], axis=0
            )
        for d in peers:
            if d:
                to = ypeer(d)
                send(vs.at[to], rv.at[NY - d], v_ss, v_rs, g, x * NY + to)
            else:
                rv[0] = vs[y]

    r32 = lax.broadcasted_iota(jnp.int32, (32, SPAN), 0)
    l32 = lax.broadcasted_iota(jnp.int32, (32, SPAN), 1)
    pick = l32 == (r32 // 16) * span + (y // 2) * 16 + r32 % 16
    arrived(rv.at[: NY - 1], v_rs)
    tops, totals = [], []
    for k in range(NY):
        three = rv[k, 32:48, :].astype(F32)
        tops.append(three[0:1] + three[1:2] + three[2:3])
        totals.append(three[3:4] + three[4:5] + three[5:6])
    peak = functools.reduce(jnp.maximum, tops)
    factors = [jnp.exp(t - peak) for t in tops]
    denom = functools.reduce(jnp.add, [f * t for f, t in zip(factors, totals)])
    shares = [
        jnp.sum(jnp.where(pick, f / denom, 0.0), axis=1, keepdims=True) for f in factors
    ]
    head = functools.reduce(
        jnp.add, [s * rv[k, :32, :].astype(F32) for k, s in enumerate(shares)]
    )
    ho[x, 0] = jnp.concatenate([head[:16], head[16:]], axis=1).astype(BF)

    def slot(r):
        return jnp.where(r < 5, jnp.maximum(2 * r - 1, 0), 2 * NY - 2 * r)

    STEPS = (0, 1, 7, 2, 6, 3, 5, 4)
    for d in FAR_Y:
        k = STEPS.index(NY - d)
        send(ho.at[x, 0], ho.at[x, k], y_ss, y_rs.at[k // 5], g, x * NY + ypeer(d))
    arrived(ho.at[x, 1:5], y_rs.at[0])
    for d in FAR_X:
        piece = ho.at[x, 0:5]
        send(piece, piece, x_ss, x_rs.at[x], g, xpeer(d) * NY + y)
    arrived(ho.at[x, 5:8], y_rs.at[1])
    for d in FAR_X:
        piece = ho.at[x, 5:8]
        send(piece, piece, x_ss, x_rs.at[x], g, xpeer(d) * NY + y)

    @pl.when(z < NG // 2 - 1)
    def _():
        pl.semaphore_wait(up_sem, NG - 2 - 2 * z)

    @pl.loop(0, NX)
    def _(xx):
        @pl.when(xx != x)
        def _():
            arrived(ho.at[xx], x_rs.at[xx])

        lhs = jnp.concatenate(
            [
                jnp.concatenate(
                    [ho[xx, slot((2 * tb + hp - y) % NY)] for hp in range(2)], axis=1
                )
                for tb in range(4)
            ],
            axis=0,
        )
        share = dot_nt(lhs, wo[...]).astype(BF)
        for tb in range(4):
            to = 4 * xx + tb
            zs[to] = share[tb * 16 : (tb + 1) * 16]

            @pl.when(to != g)
            def _():
                remote(zs.at[to], z_out.at[g], z_ss, z_rs, to, inner).start()

    z_out[g] = zs[g]
    arrived(z_out.at[: NG - 1], z_rs)
    for sent, sem in (
        (qbuf.at[: NY - 1], q_ss), (lat.at[: NX - 1, part], l_ss), (lat.at[: NX - 1, part], c_ss),
        (rv.at[: NY - 1], v_ss), (ho.at[0, : NY - 1], y_ss), (ho.at[: NX - 1], x_ss),
        (zs.at[: NG - 1], z_ss),
    ):
        remote(sent, sent, sem, q_rs, g, inner).wait_send()


def local(q, ids, limits, latent, ka, va, kd, ku, vd, vu, wo):
    args = (
        q, ids.reshape(1, -1), limits, latent.T, ka, va, kd.swapaxes(2, 3), ku,
        vd.swapaxes(2, 3), vu, wo.T,
    )
    sem = pltpu.SemaphoreType.DMA
    v = pltpu.VMEM
    parts = pl.pallas_call(
        kernel,
        out_shape=pltpu.VMEM((NG, 16, 256), BF),
        in_specs=[pl.BlockSpec(memory_space=pltpu.HBM)] * len(args),
        out_specs=pl.BlockSpec(memory_space=pltpu.VMEM),
        scratch_shapes=[
            v(q.shape, BF),
            v((TOK * HEADS, NOPE), F32),
            v((TOK * HEADS, NOPE), F32),
            v((1, ids.shape[0]), jnp.int32),
            pltpu.SMEM(limits.shape, jnp.int32),
            v((NX, LAT + ROPE, SPAN), BF),
            v(ka.shape, BF),
            v(va.shape, BF),
            v(args[6].shape, BF),
            v(ku.shape, BF),
            v(args[8].shape, BF),
            v(vu.shape, BF),
            v((256, LAT), BF),
            v((NY, 48, 128), BF),
            v((2, 2 * NY * TOK, LAT + 128), BF),
            v((NY, 48, 128), BF),
            v((NY, 48, 128), BF),
            v((NX, NY, 16, 256), BF),
            v((NG, 16, 256), BF),
            sem((len(args),)),
            *[sem] * 3,
            sem((NX,)),
            *[sem] * 5,
            sem((2,)),
            sem,
            sem((NX,)),
            *[sem] * 2,
            pltpu.SemaphoreType.REGULAR,
        ],
        compiler_params=pltpu.CompilerParams(
            collective_id=0, has_side_effects=True
        ),
    )(*args)
    return jnp.sum(parts.astype(F32), axis=0)[:, : wo.shape[1]].astype(BF)


def solution(mesh):
    in_specs = (
        P("inner", "grp", None),
        P(),
        P(),
        P("inner", None),
        P("grp", None, None),
        P("grp", None, None),
        P(None, "grp", None, None),
        P(None, "grp", None, None),
        P(None, "grp", None, None),
        P(None, "grp", None, None),
        P("grp", "inner"),
    )
    return jax.shard_map(
        local, mesh=mesh, in_specs=in_specs, out_specs=P("grp", "inner"), check_vma=False
    )
```

```python
import functools

import jax
import jax.numpy as jnp
from jax import lax
from jax.experimental import pallas as pl
from jax.experimental.pallas import tpu as pltpu
from jax.sharding import PartitionSpec as P

MESH = pl.DeviceIdType.MESH
BF, F32 = jnp.bfloat16, jnp.float32
LAT, ROPE, NOPE = 512, 64, 128
NX, NY, NG = 4, 8, 16
HEADS, TOK = 4, 8
SPAN = 128
LOG2E = 1.4426950408889634
MASKED = -30000.0 * LOG2E
FAR_Y, FAR_X = (4, 3, 5, 2, 6, 1, 7), (2, 1, 3)
SCALE = (NOPE + ROPE) ** -0.5 * LOG2E


def dot(a, b):
    return lax.dot_general(a, b, (((1,), (0,)), ((), ())), preferred_element_type=F32)


def dot_nt(a, b):
    return lax.dot_general(a, b, (((1,), (1,)), ((), ())), preferred_element_type=F32)


def kernel(
    q_hbm, ids_hbm, lim_hbm, lat_hbm, ka_hbm, va_hbm, kd_hbm, ku_hbm, vd_hbm, vu_hbm, wo_hbm,
    z_out,
    q_v, q_n, q_r, ids_v, lim_s, lat, ka, va, kd, ku, vd, vu, wo,
    qbuf, qf, vs, rv, ho, zs,
    lsem, q_ss, q_rs, l_ss, l_rs, c_ss, c_rs, v_ss, v_rs, y_ss, y_rs, x_ss, x_rs, z_ss, z_rs, up_sem,
):
    g = lax.axis_index("grp")
    inner = lax.axis_index("inner")
    x, y = inner // NY, inner % NY
    z = g // 2
    core = 2 * z + 1 - g % 2

    def ypeer(d):
        return (y + d) % NY

    def xpeer(d):
        return (x + d) % NX

    def gpeer(d):
        return (g + d) % NG

    def remote(src, dst, ss, rs, to_g, to_inner):
        return pltpu.make_async_remote_copy(
            src_ref=src, dst_ref=dst, send_sem=ss, recv_sem=rs,
            device_id=(to_g, to_inner), device_id_type=MESH,
        )

    def load(n, src, dst):
        copy = pltpu.make_async_copy(src, dst, lsem.at[n])
        copy.start()
        return copy

    def arrived(dst, rs):
        remote(dst, dst, q_ss, rs, g, inner).wait_recv()

    def send(*what):
        remote(*what).start()

    get_q = load(0, q_hbm, q_v)
    get_lat = load(1, lat_hbm, lat.at[x])
    barrier = pltpu.get_barrier_semaphore()
    for d in FAR_Y:
        pl.semaphore_signal(barrier, 1, device_id=(g, x * NY + ypeer(d)), device_id_type=MESH)
    for d in FAR_X:
        pl.semaphore_signal(barrier, 1, device_id=(g, xpeer(d) * NY + y), device_id_type=MESH)
    pl.semaphore_signal(barrier, 1, device_id=(core, inner), device_id_type=MESH)
    @pl.loop(2 * z + 2, NG)
    def _(k):
        pl.semaphore_signal(barrier, 1, device_id=(k, inner), device_id_type=MESH)

    pl.semaphore_wait(barrier, NY - 1 + NX - 1 + 1 + 2 * z)
    part = pl.ds(pl.multiple_of((g % 2) * 288, 16), 288)
    for d in FAR_X:
        send(lat_hbm.at[part], lat.at[x, part], l_ss, l_rs.at[x], g, xpeer(d) * NY + y)

    get_q.wait()
    q32 = q_v[...].astype(F32)
    for t in range(TOK):
        q_n[t * HEADS : (t + 1) * HEADS, :] = q32[t, :, :NOPE]
        q_r[t * HEADS : (t + 1) * HEADS, :ROPE] = q32[t, :, NOPE:]
    rows = [q_n[pl.ds(h, TOK, stride=HEADS), :] for h in range(HEADS)]
    ropes = [q_r[pl.ds(h, TOK, stride=HEADS), :][:, :ROPE] for h in range(HEADS)]
    rows += [jnp.concatenate(ropes[h : h + 2], axis=1) for h in (0, 2)]
    qbuf[y] = jnp.concatenate(rows, axis=0).astype(BF)
    for d in FAR_Y:
        send(qbuf.at[y], qbuf.at[y], q_ss, q_rs, g, x * NY + ypeer(d))
    @pl.loop(0, 2 * z)
    def _(k):
        pl.semaphore_signal(up_sem, 1, device_id=(k, inner), device_id_type=MESH)

    get = [
        load(n + 2, src, dst)
        for n, (src, dst) in enumerate((
            (ids_hbm, ids_v), (lim_hbm, lim_s), (ka_hbm, ka), (kd_hbm, kd), (ku_hbm, ku), (va_hbm, va),
            (vd_hbm, vd), (vu_hbm, vu), (wo_hbm, wo.at[: wo_hbm.shape[0]]),
        ))
    ]

    wo[wo_hbm.shape[0] :, :] = jnp.zeros((wo.shape[0] - wo_hbm.shape[0], LAT), BF)
    for copy in [get_lat] + get:
        copy.wait()
    span = NY * TOK
    wide = NX * span
    row = lax.broadcasted_iota(jnp.int32, (span, wide), 0)
    lane = lax.broadcasted_iota(jnp.int32, (span, wide), 1)
    tenant = jnp.sum(jnp.where(lane == row + x * span, ids_v[...], 0), axis=1, keepdims=True)
    limit = jnp.zeros_like(tenant)
    for k in range(4):
        limit = jnp.where(tenant == k, lim_s[k], limit)
    chosen = lax.broadcasted_iota(jnp.int32, (span, 64), 1) // 16 == tenant

    arrived(qbuf.at[: NY - 1], q_rs)
    for d in (1, 3, 2):
        piece = lat.at[xpeer(d), part]
        arrived(piece, l_rs.at[xpeer(d)])
        send(piece, piece, c_ss, c_rs, core, inner)

    blocks = [qbuf[k].astype(F32) for k in range(NY)]
    half = lax.broadcasted_iota(jnp.int32, (span, NOPE), 1) // ROPE
    for h in range(HEADS):
        nope = jnp.concatenate([b[h * TOK : (h + 1) * TOK] for b in blocks], axis=0).astype(BF)
        first = HEADS * TOK + (h // 2) * TOK
        rope = jnp.concatenate([b[first : first + TOK] for b in blocks], axis=0)
        low = dot_nt(nope, kd[:, h].reshape(64, NOPE))
        low = jnp.where(chosen, low, 0.0).astype(BF)
        latent = dot(nope, ka[h]) + dot(low, ku[:, h].reshape(64, LAT))
        rows = pl.ds((h % 2) * span, span)
        qf[h // 2, rows, :LAT] = latent.astype(BF)
        qf[h // 2, rows, LAT:] = jnp.where(half == h % 2, rope, 0.0).astype(BF)

    other = pl.ds(pl.multiple_of((1 - g % 2) * 288, 16), 288)
    arrived(lat.at[: NX - 1, other], c_rs)

    base = lax.broadcasted_iota(jnp.int32, (2 * span, SPAN), 1) + y * SPAN
    limit2 = jnp.concatenate([limit, limit], axis=0)
    eye = lax.broadcasted_iota(jnp.int32, (SPAN, SPAN), 0) == lax.broadcasted_iota(
        jnp.int32, (SPAN, SPAN), 1
    )
    okay = [base + b * NY * SPAN < limit2 for b in range(NX)]
    for turn, peers in enumerate(((4, 2, 6, 0), (3, 5, 1, 7))):
        hp = (y + turn) % 2
        mine = qf[hp]
        scores = []
        for b in range(NX):
            keys = jnp.concatenate([lat[b], lat[b, LAT:]], axis=0)
            scores.append(jnp.where(okay[b], dot(mine, keys) * SCALE, MASKED))
        top = functools.reduce(jnp.maximum, scores)
        top = jnp.max(top, axis=1, keepdims=True)
        weights = [jnp.where(ok, jnp.exp2(s - top), 0.0) for ok, s in zip(okay, scores)]
        total = jnp.sum(functools.reduce(jnp.add, weights), axis=1, keepdims=True)
        acc = functools.reduce(
            jnp.add, [dot_nt(w.astype(BF), lat[b, :LAT]) for b, w in enumerate(weights)]
        ).astype(BF)
        three = []
        for column in (top, total):
            rest = jnp.sum(jnp.where(eye, column, 0.0), axis=0, keepdims=True)
            for _ in range(3):
                three.append(rest.astype(BF).astype(F32))
                rest = rest - three[-1]
        three = jnp.concatenate(three + [jnp.zeros((10, SPAN), F32)], axis=0).astype(BF)
        values = []
        for hl in range(2):
            h = hp * 2 + hl
            mine = acc[hl * span : (hl + 1) * span, :]
            low = dot_nt(mine, vd[:, h].reshape(64, LAT))
            low = jnp.where(chosen, low, 0.0).astype(BF)
            values.append((dot(mine, va[h]) + dot(low, vu[:, h].reshape(64, NOPE))).astype(BF))
        for tb in range(4):
            vs[tb * 2 + hp] = jnp.concatenate(
                [values[0][tb * 16 : (tb + 1) * 16], values[1][tb * 16 : (tb + 1) * 16], three], axis=0
            )
        for d in peers:
            if d:
                to = ypeer(d)
                send(vs.at[to], rv.at[NY - d], v_ss, v_rs, g, x * NY + to)
            else:
                rv[0] = vs[y]

    r32 = lax.broadcasted_iota(jnp.int32, (32, SPAN), 0)
    l32 = lax.broadcasted_iota(jnp.int32, (32, SPAN), 1)
    pick = l32 == (r32 // 16) * span + (y // 2) * 16 + r32 % 16
    arrived(rv.at[: NY - 1], v_rs)
    tops, totals = [], []
    for k in range(NY):
        three = rv[k, 32:48, :].astype(F32)
        tops.append(three[0:1] + three[1:2] + three[2:3])
        totals.append(three[3:4] + three[4:5] + three[5:6])
    peak = functools.reduce(jnp.maximum, tops)
    factors = [jnp.exp2(t - peak) for t in tops]
    denom = functools.reduce(jnp.add, [f * t for f, t in zip(factors, totals)])
    shares = [
        jnp.sum(jnp.where(pick, f / denom, 0.0), axis=1, keepdims=True) for f in factors
    ]
    head = functools.reduce(
        jnp.add, [s * rv[k, :32, :].astype(F32) for k, s in enumerate(shares)]
    )
    ho[x, 0] = jnp.concatenate([head[:16], head[16:]], axis=1).astype(BF)

    def slot(r):
        return jnp.where(r < 5, jnp.maximum(2 * r - 1, 0), 2 * NY - 2 * r)

    STEPS = (0, 1, 7, 2, 6, 3, 5, 4)
    for d in FAR_Y:
        k = STEPS.index(NY - d)
        send(ho.at[x, 0], ho.at[x, k], y_ss, y_rs.at[k // 5], g, x * NY + ypeer(d))
    arrived(ho.at[x, 1:5], y_rs.at[0])
    for d in FAR_X:
        piece = ho.at[x, 0:5]
        send(piece, piece, x_ss, x_rs.at[x], g, xpeer(d) * NY + y)
    arrived(ho.at[x, 5:8], y_rs.at[1])
    for d in FAR_X:
        piece = ho.at[x, 5:8]
        send(piece, piece, x_ss, x_rs.at[x], g, xpeer(d) * NY + y)

    @pl.when(z < NG // 2 - 1)
    def _():
        pl.semaphore_wait(up_sem, NG - 2 - 2 * z)

    @pl.loop(0, NX)
    def _(xx):
        @pl.when(xx != x)
        def _():
            arrived(ho.at[xx], x_rs.at[xx])

        lhs = jnp.concatenate(
            [
                jnp.concatenate(
                    [ho[xx, slot((2 * tb + hp - y) % NY)] for hp in range(2)], axis=1
                )
                for tb in range(4)
            ],
            axis=0,
        )
        share = dot_nt(lhs, wo[...]).astype(BF)
        for tb in range(4):
            to = 4 * xx + tb
            zs[to] = share[tb * 16 : (tb + 1) * 16]

            @pl.when(to != g)
            def _():
                remote(zs.at[to], z_out.at[g], z_ss, z_rs, to, inner).start()

    z_out[g] = zs[g]
    arrived(z_out.at[: NG - 1], z_rs)
    for sent, sem in (
        (qbuf.at[: NY - 1], q_ss), (lat.at[: NX - 1, part], l_ss), (lat.at[: NX - 1, part], c_ss),
        (rv.at[: NY - 1], v_ss), (ho.at[0, : NY - 1], y_ss), (ho.at[: NX - 1], x_ss),
        (zs.at[: NG - 1], z_ss),
    ):
        remote(sent, sent, sem, q_rs, g, inner).wait_send()


def local(q, ids, limits, latent, ka, va, kd, ku, vd, vu, wo):
    args = (
        q, ids.reshape(1, -1), limits, latent.T, ka, va, kd.swapaxes(2, 3), ku,
        vd.swapaxes(2, 3), vu, wo.T,
    )
    sem = pltpu.SemaphoreType.DMA
    v = pltpu.VMEM
    parts = pl.pallas_call(
        kernel,
        out_shape=pltpu.VMEM((NG, 16, 256), BF),
        in_specs=[pl.BlockSpec(memory_space=pltpu.HBM)] * len(args),
        out_specs=pl.BlockSpec(memory_space=pltpu.VMEM),
        scratch_shapes=[
            v(q.shape, BF),
            v((TOK * HEADS, NOPE), F32),
            v((TOK * HEADS, NOPE), F32),
            v((1, ids.shape[0]), jnp.int32),
            pltpu.SMEM(limits.shape, jnp.int32),
            v((NX, LAT + ROPE, SPAN), BF),
            v(ka.shape, BF),
            v(va.shape, BF),
            v(args[6].shape, BF),
            v(ku.shape, BF),
            v(args[8].shape, BF),
            v(vu.shape, BF),
            v((256, LAT), BF),
            v((NY, 48, 128), BF),
            v((2, 2 * NY * TOK, LAT + 128), BF),
            v((NY, 48, 128), BF),
            v((NY, 48, 128), BF),
            v((NX, NY, 16, 256), BF),
            v((NG, 16, 256), BF),
            sem((len(args),)),
            *[sem] * 3,
            sem((NX,)),
            *[sem] * 5,
            sem((2,)),
            sem,
            sem((NX,)),
            *[sem] * 2,
            pltpu.SemaphoreType.REGULAR,
        ],
        compiler_params=pltpu.CompilerParams(
            collective_id=0, has_side_effects=True
        ),
    )(*args)
    return jnp.sum(parts.astype(F32), axis=0)[:, : wo.shape[1]].astype(BF)


def solution(mesh):
    in_specs = (
        P("inner", "grp", None),
        P(),
        P(),
        P("inner", None),
        P("grp", None, None),
        P("grp", None, None),
        P(None, "grp", None, None),
        P(None, "grp", None, None),
        P(None, "grp", None, None),
        P(None, "grp", None, None),
        P("grp", "inner"),
    )
    return jax.shard_map(
        local, mesh=mesh, in_specs=in_specs, out_specs=P("grp", "inner"), check_vma=False
    )
```
